128 devices in a mesh: ctx: 16 (over x_lo, z, core), head: 8 (over x_hi, y).
Axes of the slice: x: 4 (x_hi: 2, x_lo: 2; x = x_hi * 2 + x_lo), y: 4, z: 4, core: 2. Of those that a mesh axis runs over, the one named last changes fastest.
Arguments:
- queries: bfloat16 [1024, 8192], P('ctx', 'head'), may hold values from -40 to 40
- stretch_keys: bfloat16 [1024, 1024], P('ctx', 'head'), may hold values from -4 to 4
- stretch_values: bfloat16 [1024, 1024], P('ctx', 'head'), may hold values from -5 to 5
- cache_keys: bfloat16 [32768, 1024], P('ctx', 'head'), may hold values from -4 to 4
- cache_values: bfloat16 [32768, 1024], P('ctx', 'head'), may hold values from -5 to 5
- head_types: int32 [8], replicated, may hold values from 0 to 1, as said below
- sink_blocks: int32 [8], replicated, may hold values from 1 to 4, as said below
- window_blocks: int32 [8], replicated, may hold values from 1 to 8, as said below
Outputs:
- attended: bfloat16 [1024, 8192], P('ctx', 'head')
The draws below stay inside these ranges and needn't reach their ends.
Inputs may be any that keep to these rules, and one draw needn't show every extreme that they name: `head_types`: exactly half of the 8 heads are retrieval heads. `sink_blocks`: some head has 4. `window_blocks`: some head has 8.
All inputs are finite; a program needn't handle non-finite values.
Results may differ from the reference program's by a relative error of at most 0.0044.
Values may be sent and summed in bfloat16 or wider, within the bound.
No kernel may reach another device: no remote copies, remote signals or barrier semaphores. Data moves between devices by JAX's collectives and lax.ppermute only.
A program may use at most 64 MiB of HBM per device.

```python
import jax
import jax.numpy as jnp
from jax import lax

HEADS_Q = 64
KV_HEADS = 8
D_HEAD = 128
SINK_MAX = 4
WIN_MAX = 8
CONTEXT = 32768
STRETCH = 1024


def draw_cache_keys(key, part):
    key = jax.random.fold_in(key, 3)
    drawn = jnp.clip(jax.random.normal(key, (CONTEXT, KV_HEADS * D_HEAD), jnp.float32), -4.0, 4.0)
    return drawn.astype(jnp.bfloat16)


def draw_queries(key, part):
    key = jax.random.fold_in(key, 4)
    row_width = HEADS_Q * D_HEAD
    drawn = jnp.clip(3.0 * jax.random.normal(key, (STRETCH, row_width), jnp.float32), -12.0, 12.0)
    return drawn.astype(jnp.bfloat16)


def draw_head_types(key, part):
    key = jax.random.fold_in(key, 8)
    order = jax.random.permutation(key, KV_HEADS)
    return (order < KV_HEADS // 2).astype(jnp.int32)


def bounded_counts(key, upper):
    first_key, second_key = jax.random.split(key)
    drawn = jax.random.randint(first_key, (KV_HEADS,), 1, upper + 1)
    chosen = jax.random.randint(second_key, (), 0, KV_HEADS)
    return jnp.where(jnp.arange(KV_HEADS) == chosen, upper, drawn).astype(jnp.int32)


def draw_sink_blocks(key, part):
    key = jax.random.fold_in(key, 5)
    return bounded_counts(key, SINK_MAX)


def draw_window_blocks(key, part):
    key = jax.random.fold_in(key, 6)
    return bounded_counts(key, WIN_MAX)


def block_levels(stream_key, extent, pieces, smallest, top_value):
    def one(position, shards_of):
        draws = jax.random.uniform(jax.random.fold_in(jax.random.fold_in(stream_key, 6), position), (shards_of,), jnp.float32, smallest / len(pieces), top_value / len(pieces))
        return jnp.repeat(jnp.exp(draws), extent[position] // shards_of).reshape((-1,) + (1,) * (len(extent) - position - 1))

    loudness = one(*pieces[0])
    for cut in pieces[1:]:
        loudness = loudness * one(*cut)
    return loudness


def gaussian(key, dims, width, reach, cuts=(), kind=jnp.bfloat16):
    level = block_levels(key, dims, cuts, -0.22, 0.18) if cuts else 1.0
    values = jax.random.normal(key, dims, jnp.float32) * width * level
    return jnp.minimum(jnp.maximum(values, -reach), reach).astype(kind)


def setup_inputs(seed: int = 0) -> dict:
    key_of = jax.random.split(jax.random.key(seed), 9)
    queries = draw_queries(jax.random.fold_in(key_of[8], 71), 0)
    stretch_keys = gaussian(key_of[1], (STRETCH, KV_HEADS * D_HEAD), 1.0, 4.0, ((0, 16), (1, 8)))
    stretch_values = gaussian(key_of[2], (STRETCH, KV_HEADS * D_HEAD), 1.0, 5.0, ((0, 16), (1, 8)))
    cache_keys = draw_cache_keys(jax.random.fold_in(key_of[8], 71), 0)
    cache_values = gaussian(key_of[4], (CONTEXT, KV_HEADS * D_HEAD), 1.0, 5.0, ((0, 16), (1, 8)))
    head_types = draw_head_types(jax.random.fold_in(key_of[8], 71), 0)
    sink_blocks = draw_sink_blocks(jax.random.fold_in(key_of[8], 71), 0)
    window_blocks = draw_window_blocks(jax.random.fold_in(key_of[8], 71), 0)
    return {"queries": queries, "stretch_keys": stretch_keys, "stretch_values": stretch_values, "cache_keys": cache_keys, "cache_values": cache_values, "head_types": head_types, "sink_blocks": sink_blocks, "window_blocks": window_blocks}


neg_fill = -1.0e30


def kept_flags(key_pos, context, head_kind, sink_count, window_count):
    return ((head_kind == 1) | (key_pos < 128 * sink_count)
            | ((key_pos >= context - 128 * window_count) & (key_pos < context))
            | (key_pos >= context))


def reference(queries, stretch_keys, stretch_values, cache_keys, cache_values, head_types, sink_blocks, window_blocks):
    context = cache_keys.shape[0]
    stretch_len = queries.shape[0]
    group_size = HEADS_Q // KV_HEADS
    score_scale = 1.0 / (D_HEAD ** 0.5)
    key_span = 2048 if context % 2048 == 0 else 256
    block_count = context // key_span
    query_pos = context + jnp.arange(stretch_len, dtype=jnp.int32)

    def one_head(head_index):
        query_head = lax.dynamic_slice_in_dim(queries, head_index * group_size * D_HEAD, group_size * D_HEAD, 1)
        query_head = query_head.reshape(stretch_len, group_size, D_HEAD).astype(jnp.float32)
        cache_k = lax.dynamic_slice_in_dim(cache_keys, head_index * D_HEAD, D_HEAD, 1)
        cache_v = lax.dynamic_slice_in_dim(cache_values, head_index * D_HEAD, D_HEAD, 1)
        own_k = lax.dynamic_slice_in_dim(stretch_keys, head_index * D_HEAD, D_HEAD, 1)
        own_v = lax.dynamic_slice_in_dim(stretch_values, head_index * D_HEAD, D_HEAD, 1)
        head_kind = head_types[head_index]
        sink_count = sink_blocks[head_index]
        window_count = window_blocks[head_index]

        def scores_allowed(key_block, key_pos):
            scores = jnp.einsum("qgd,rd->qgr", query_head, key_block.astype(jnp.float32)) * score_scale
            allowed = kept_flags(key_pos, context, head_kind, sink_count, window_count)
            allowed = allowed[None, None, :] & (key_pos[None, None, :] <= query_pos[:, None, None])
            return scores, allowed

        def block_max(running, key_block, key_pos):
            scores, allowed = scores_allowed(key_block, key_pos)
            return jnp.maximum(running, jnp.max(jnp.where(allowed, scores, neg_fill), axis=2))

        def block_sums(running, key_block, value_block, key_pos, row_max):
            scores, allowed = scores_allowed(key_block, key_pos)
            weights = jnp.where(allowed, jnp.exp(scores - row_max[:, :, None]), 0.0)
            weights16 = weights.astype(jnp.bfloat16).astype(jnp.float32)
            numerator = running[0] + jnp.einsum("qgr,rd->qgd", weights16, value_block.astype(jnp.float32))
            return (numerator, running[1] + jnp.sum(weights, axis=2))

        def cache_pos(block_index):
            return block_index * key_span + jnp.arange(key_span, dtype=jnp.int32)

        def max_step(block_index, running):
            key_pos = cache_pos(block_index)
            key_block = lax.dynamic_slice_in_dim(cache_k, block_index * key_span, key_span, 0)
            needed = jnp.any(kept_flags(key_pos, context, head_kind, sink_count, window_count))
            return lax.cond(needed, lambda current: block_max(current, key_block, key_pos), lambda current: current, running)

        row_max = jnp.full((stretch_len, group_size), neg_fill, jnp.float32)
        row_max = lax.fori_loop(0, block_count, max_step, row_max)
        row_max = block_max(row_max, own_k, query_pos)

        def sum_step(block_index, running):
            key_pos = cache_pos(block_index)
            key_block = lax.dynamic_slice_in_dim(cache_k, block_index * key_span, key_span, 0)
            value_block = lax.dynamic_slice_in_dim(cache_v, block_index * key_span, key_span, 0)
            needed = jnp.any(kept_flags(key_pos, context, head_kind, sink_count, window_count))
            return lax.cond(needed, lambda current: block_sums(current, key_block, value_block, key_pos, row_max),
                            lambda current: current, running)

        totals = (jnp.zeros((stretch_len, group_size, D_HEAD), jnp.float32), jnp.zeros((stretch_len, group_size), jnp.float32))
        totals = lax.fori_loop(0, block_count, sum_step, totals)
        totals = block_sums(totals, own_k, own_v, query_pos, row_max)
        result = totals[0] / totals[1][:, :, None]
        return result.reshape(stretch_len, group_size * D_HEAD).astype(jnp.bfloat16)

    stacked = lax.map(one_head, jnp.arange(KV_HEADS, dtype=jnp.int32))
    return jnp.transpose(stacked, (1, 0, 2)).reshape(stretch_len, HEADS_Q * D_HEAD)
```

```python
import functools
import math

import jax
import jax.numpy as jnp
from jax import lax
from jax.experimental import pallas as pl
from jax.experimental.pallas import tpu as pltpu
from jax.sharding import PartitionSpec as P

D = 128
BLOCK = 128
SCALE = math.log2(math.e) / math.sqrt(D)
NEG = -1e30
HEADROOM = 40.0
SAFE = 2.0**100
SAMPLE = 256
NT = (((1,), (1,)), ((), ()))
F32 = jnp.float32
BF16 = jnp.bfloat16


def scores_of(query, keys):
    return lax.dot_general(query, keys, NT, preferred_element_type=F32)


def row_max(x):
    peak = functools.reduce(
        jnp.maximum, [x[:, i : i + D] for i in range(0, x.shape[1], D)]
    )
    return jnp.broadcast_to(jnp.max(peak, axis=1, keepdims=True), (x.shape[0], D))


def attend_kernel(geom, *refs):
    (steps, flips, rows, own, first, shard, ctx_count, state_in, emit) = geom
    n, n_src = len(steps), len(flips)
    it = iter(refs)
    kinds, sinks, windows = next(it), next(it), next(it)
    q_in = [next(it) for _ in range(n)]
    kv_in = [next(it) for _ in range(n_src)]
    st_in = [next(it) for _ in range(len(state_in))]
    out = [next(it) for _ in range(n)] if emit else [next(it)]
    q_buf, kv_buf, state, message, in_sem, out_sem = it

    group = q_in[0].shape[1] // D
    tokens = q_in[0].shape[0]
    q_rows = group * tokens
    ctx = lax.axis_index("ctx")
    head = lax.axis_index("head")
    kind = kinds[head]
    sink = sinks[head]
    window = windows[head]
    total_blocks = ctx_count * shard // BLOCK

    copies = [
        pltpu.make_async_copy(kv_in[s], kv_buf.at[s], in_sem.at[s]) for s in range(n_src)
    ]
    place = 0
    for i, (ref, which) in enumerate(zip(st_in, state_in)):
        for j in which:
            copies.append(
                pltpu.make_async_copy(ref.at[j], state.at[place], in_sem.at[n_src + place])
            )
            place += 1
    for copy in copies:
        copy.start()
    for c in range(n):
        for g in range(group):
            q_buf[c, g * tokens : (g + 1) * tokens, :] = q_in[c][:, g * D : (g + 1) * D]
    for copy in copies:
        copy.wait()

    k_stretch = rows
    v_cache = rows + own
    v_stretch = 2 * rows + own

    if own:
        column = lax.broadcasted_iota(jnp.int32, (q_rows, n_src * own), 1)
        row = lax.broadcasted_iota(jnp.int32, (q_rows, n_src * own), 0)
        key_pos = jnp.zeros_like(column)
        for s in range(n_src):
            key_pos = jnp.where(
                (column >= s * own) & (column < (s + 1) * own),
                (ctx ^ flips[s]) * own + column - s * own,
                key_pos,
            )
        token = row % tokens

    def stretch_parts(c):
        keys = jnp.concatenate(
            [kv_buf[s, k_stretch : k_stretch + own, :] for s in range(n_src)], 0
        )
        values = jnp.concatenate(
            [kv_buf[s, v_stretch : v_stretch + own, :] for s in range(n_src)], 0
        )
        x = scores_of(q_buf[c], keys) * SCALE
        owner = jnp.int32(0)
        for i, step in enumerate(steps):
            owner = jnp.where(c == i, source_of(ctx, step), owner)
        return x, values, key_pos <= token + owner * tokens

    def one_chunk(c, _):
        if not state_in:
            state[c, 1] = jnp.zeros((q_rows, D), F32)
            state[c, 2] = jnp.zeros((q_rows, D), F32)

            @pl.when(kind == 1)
            def _():
                sample = scores_of(q_buf[c], kv_buf[0, :SAMPLE, :])
                state[c, 0] = row_max(sample) * SCALE + HEADROOM

            @pl.when(kind != 1)
            def _():
                state[c, 0] = jnp.full((q_rows, D), NEG, F32)

        def exact():
            def update(x, values, mask):
                old = state[c, 0]
                if mask is not None:
                    x = jnp.where(mask, x, NEG)
                new = jnp.maximum(old, row_max(x))
                fade = jnp.exp2(old - new)
                p = jnp.exp2(x - new)
                if mask is not None:
                    p = jnp.where(mask, p, 0.0)
                state[c, 0] = new
                state[c, 1] = state[c, 1] * fade + p
                state[c, 2] = state[c, 2] * fade + jnp.dot(
                    p.astype(BF16), values, preferred_element_type=F32
                )

            for s in range(n_src):
                base = ((ctx ^ flips[s]) * shard + first) // BLOCK
                blocks = rows // BLOCK
                low = jnp.where(kind == 1, blocks, jnp.clip(sink - base, 0, blocks))
                high = jnp.clip(total_blocks - window - base, low, blocks)

                def step(j, _, s=s):
                    at = pl.multiple_of(j * BLOCK, BLOCK)
                    x = scores_of(q_buf[c], kv_buf[s, pl.ds(at, BLOCK), :]) * SCALE
                    update(x, kv_buf[s, pl.ds(v_cache + at, BLOCK), :], None)
                    return 0

                lax.fori_loop(0, low, step, 0)
                lax.fori_loop(high, blocks, step, 0)
            if own:
                update(*stretch_parts(c))

        @pl.when(kind == 1)
        def _():
            fixed = state[c, 0]

            def source(s, carry):
                total, acc = carry
                x = scores_of(q_buf[c], kv_buf[s, :rows, :])
                weights = []
                for i in range(0, rows, D):
                    p = jnp.exp2(x[:, i : i + D] * SCALE - fixed)
                    total = total + p
                    weights.append(p.astype(BF16))
                acc = acc + jnp.dot(
                    jnp.concatenate(weights, 1),
                    kv_buf[s, v_cache : v_cache + rows, :],
                    preferred_element_type=F32,
                )
                return total, acc

            total, acc = lax.fori_loop(0, n_src, source, (state[c, 1], state[c, 2]))
            if own:
                x, values, mask = stretch_parts(c)
                p = jnp.where(mask, jnp.exp2(x - fixed), 0.0)
                total = total + p
                acc = acc + jnp.dot(p.astype(BF16), values, preferred_element_type=F32)
            safe = jnp.min(jnp.where(total < SAFE, 1.0, 0.0)) > 0.5

            @pl.when(safe)
            def _():
                state[c, 1] = total
                state[c, 2] = acc

            @pl.when(jnp.logical_not(safe))
            def _():
                exact()

        @pl.when(kind != 1)
        def _():
            exact()

        if emit:
            total = jnp.sum(state[c, 1], axis=1, keepdims=True)
            some = total > 0.0
            total = jnp.where(some, total, 1.0)
            part = state[c, 2] / total
            message[c, :q_rows, :] = part.astype(BF16)
            log_sum = jnp.where(some, state[c, 0] + jnp.log(total) * math.log2(math.e), NEG)
            eye = lax.broadcasted_iota(jnp.int32, (D, D), 0) == lax.broadcasted_iota(
                jnp.int32, (D, D), 1
            )
            lines = []
            for i in range(0, q_rows, D):
                lines.append(
                    jnp.sum(jnp.where(eye, log_sum[i : i + D, :], 0.0), axis=0, keepdims=True)
                )
            lines = jnp.concatenate(lines, 0)
            pieces = []
            for _ in range(3):
                piece = lines.astype(BF16).astype(F32)
                pieces.append(piece)
                lines = lines - piece
            pad = 16 - 3 * (q_rows // D)
            tail = jnp.concatenate(pieces + [jnp.zeros((pad, D), F32)], 0)
            message[c, q_rows:, :] = tail.astype(BF16)
        return 0

    if n == 1:
        one_chunk(0, 0)
    else:
        lax.fori_loop(0, n, one_chunk, 0)
    if emit:
        copies = [
            pltpu.make_async_copy(message.at[c], out[c], out_sem.at[c]) for c in range(n)
        ]
    else:
        copies = [
            pltpu.make_async_copy(state.at[c], out[0].at[c], out_sem.at[c]) for c in range(n)
        ]
    for copy in copies:
        copy.start()
    for copy in copies:
        copy.wait()


def source_of(ctx, step):
    return (ctx // 8) * 8 + (ctx % 8 - 2 * step + 8) % 8


def attend(tables, queries, steps, sources, flips, rows, own, first, shard, states, emit):
    n, n_src = len(steps), len(flips)
    tokens, width = queries[0].shape
    q_rows = tokens * (width // D)
    ctx_count = lax.axis_size("ctx")
    geom = (
        tuple(steps),
        tuple(flips),
        rows,
        own,
        first,
        shard,
        ctx_count,
        tuple(tuple(which) for _, which in states),
        emit,
    )
    if emit:
        out_shape = [jax.ShapeDtypeStruct((q_rows + 16, D), BF16)] * n
    else:
        out_shape = [jax.ShapeDtypeStruct((n, 3, q_rows, D), F32)]
    smem = pl.BlockSpec(memory_space=pltpu.SMEM)
    vmem = pl.BlockSpec(memory_space=pltpu.VMEM)
    anywhere = pl.BlockSpec(memory_space=pl.ANY)
    pairs = n * q_rows * n_src * (rows + own)
    outs = pl.pallas_call(
        functools.partial(attend_kernel, geom),
        out_shape=out_shape,
        in_specs=[smem] * 3 + [vmem] * n + [anywhere] * (n_src + len(states)),
        out_specs=[anywhere] * len(out_shape),
        scratch_shapes=[
            pltpu.VMEM((n, q_rows, D), BF16),
            pltpu.VMEM((n_src,) + sources[0].shape, BF16),
            pltpu.VMEM((n, 3, q_rows, D), F32),
            pltpu.VMEM((n if emit else 1, q_rows + 16, D), BF16),
            pltpu.SemaphoreType.DMA((n_src + n,)),
            pltpu.SemaphoreType.DMA((n,)),
        ],
        compiler_params=pltpu.CompilerParams(vmem_limit_bytes=40 * 2**20),
        cost_estimate=pl.CostEstimate(
            flops=4 * pairs * D, bytes_accessed=2 * n_src * rows * 2 * D, transcendentals=pairs
        ),
    )(*tables, *queries, *sources, *[array for array, _ in states])
    return outs if emit else outs[0]


def combine_kernel(*refs):
    *parts, out = refs
    tokens, width = out.shape
    group = width // D
    q_rows = tokens * group
    for i in range(q_rows // D):
        logs = []
        for part in parts:
            tail = part[q_rows:, :].astype(F32)
            step = q_rows // D
            logs.append(
                tail[i : i + 1] + tail[step + i : step + i + 1] + tail[2 * step + i : 2 * step + i + 1]
            )
        peak = functools.reduce(jnp.maximum, logs)
        weights = [jnp.exp2(x - peak) for x in logs]
        total = functools.reduce(jnp.add, weights)
        acc = jnp.zeros((D, D), F32)
        for part, weight in zip(parts, weights):
            spread = jnp.broadcast_to(weight / total, (D, D)).T
            acc = acc + spread * part[i * D : (i + 1) * D, :].astype(F32)
        for j in range(D // tokens):
            g = i * (D // tokens) + j
            out[:, g * D : (g + 1) * D] = acc[j * tokens : (j + 1) * tokens].astype(BF16)


def combine(parts, tokens, width):
    return pl.pallas_call(
        combine_kernel,
        out_shape=jax.ShapeDtypeStruct((tokens, width), BF16),
        compiler_params=pltpu.CompilerParams(vmem_limit_bytes=16 * 2**20),
    )(*parts)


def flip_perm(count, bits):
    return [(i, i ^ bits) for i in range(count)]


def step_perm(count, step):
    return [(i, (i // 8) * 8 + (i % 8 + 2 * step) % 8) for i in range(count)]


def local(
    queries, stretch_keys, stretch_values, cache_keys, cache_values, head_types, sink_blocks, window_blocks
):
    count = lax.axis_size("ctx")
    tables = (head_types, sink_blocks, window_blocks)
    tokens, width = queries.shape
    shard = cache_keys.shape[0]
    own = stretch_keys.shape[0]

    def send(x, perm):
        return lax.ppermute(x, "ctx", perm)

    packed = jnp.concatenate([cache_keys, stretch_keys, cache_values, stretch_values], 0)
    far = send(packed, flip_perm(count, 8))
    steps = [0, 1, 3, 2]
    chunks = [queries] + [send(queries, step_perm(count, s)) for s in steps[1:]]
    sibling = send(packed, flip_perm(count, 1))

    def call(which, sources, flips, states, emit):
        return attend(
            tables,
            [chunks[i] for i in which],
            [steps[i] for i in which],
            sources,
            flips,
            shard,
            own,
            0,
            shard,
            states,
            emit,
        )

    near = [packed, sibling]
    state0 = call([0], near, [0, 1], [], False)
    state1 = call([1, 2, 3], near, [0, 1], [], False)
    far, state0, state1 = lax.optimization_barrier((far, state0, state1))
    far_sibling = send(far, flip_perm(count, 1))
    parts = call(
        [0, 1, 2, 3], [far, far_sibling], [8, 9], [(state0, [0]), (state1, [0, 1, 2])], True
    )
    back = [parts[0]] + [
        send(part, step_perm(count, -s)) for part, s in zip(parts[1:], steps[1:])
    ]
    return combine(back, tokens, width)


def solution(mesh):
    placed = (
        P("ctx", "head"),
        P("ctx", "head"),
        P("ctx", "head"),
        P("ctx", "head"),
        P("ctx", "head"),
        P(),
        P(),
        P(),
    )
    return jax.shard_map(
        local, mesh=mesh, in_specs=placed, out_specs=P("ctx", "head"), check_vma=False
    )
```

```python
import functools
import math

import jax
import jax.numpy as jnp
from jax import lax
from jax.experimental import pallas as pl
from jax.experimental.pallas import tpu as pltpu
from jax.sharding import PartitionSpec as P

D = 128
BLOCK = 128
SCALE = math.log2(math.e) / math.sqrt(D)
NEG = -1e30
HEADROOM = 40.0
SAFE = 2.0**100
SAMPLE = 256
CUT = 1536
SEGMENT = 512
VMEM_LIMIT = 32 * 2**20
NT = (((1,), (1,)), ((), ()))
F32 = jnp.float32
BF16 = jnp.bfloat16


def scores_of(query, keys):
    return lax.dot_general(query, keys, NT, preferred_element_type=F32)


def row_max(x):
    peak = functools.reduce(
        jnp.maximum, [x[:, i : i + D] for i in range(0, x.shape[1], D)]
    )
    return jnp.broadcast_to(jnp.max(peak, axis=1, keepdims=True), (x.shape[0], D))


def attend_kernel(geom, *refs):
    steps, sources, shard, ctx_count, state_in, emit = geom
    n, n_src = len(steps), len(sources)
    kinds, sinks, windows = refs[:3]
    q_in = refs[3 : 3 + n]
    kv = refs[3 + n : 3 + n + n_src]
    rest = refs[3 + n + n_src :]
    if state_in:
        old, rest = rest[0], rest[1:]
    out, q_buf = rest[0], rest[1]
    state = rest[2] if emit else out
    group = q_in[0].shape[1] // D
    tokens = q_in[0].shape[0]
    q_rows = group * tokens
    ctx = lax.axis_index("ctx")
    head = lax.axis_index("head")
    kind = kinds[head]
    sink = sinks[head]
    window = windows[head]
    total_blocks = ctx_count * shard // BLOCK

    for c in range(n):
        for g in range(group):
            q_buf[c, g * tokens : (g + 1) * tokens, :] = q_in[c][:, g * D : (g + 1) * D]
    with_stretch = [s for s in range(n_src) if sources[s][2]]
    if with_stretch:
        own = sources[with_stretch[0]][2]
        wide = len(with_stretch) * own
        column = lax.broadcasted_iota(jnp.int32, (q_rows, wide), 1)
        token = lax.broadcasted_iota(jnp.int32, (q_rows, wide), 0) % tokens
        key_pos = jnp.zeros_like(column)
        for i, s in enumerate(with_stretch):
            here = (column >= i * own) & (column < (i + 1) * own)
            key_pos = jnp.where(here, (ctx ^ sources[s][0]) * own + column - i * own, key_pos)

    def stretch_parts(c):
        keys, values = [], []
        for s in with_stretch:
            rows = sources[s][1]
            keys.append(kv[s][rows : rows + own, :])
            values.append(kv[s][2 * rows + own : 2 * rows + 2 * own, :])
        owner = jnp.int32(0)
        for i, step in enumerate(steps):
            owner = jnp.where(c == i, source_of(ctx, step), owner)
        x = scores_of(q_buf[c], jnp.concatenate(keys, 0)) * SCALE
        return x, jnp.concatenate(values, 0), key_pos <= token + owner * tokens

    def exact(c):
        if state_in:
            for i in range(3):
                state[c, i] = old[c, i]
        else:
            state[c, 0] = jnp.full((q_rows, D), NEG, F32)
            state[c, 1] = jnp.zeros((q_rows, D), F32)
            state[c, 2] = jnp.zeros((q_rows, D), F32)

        def update(x, values, mask):
            before = state[c, 0]
            if mask is not None:
                x = jnp.where(mask, x, NEG)
            now = jnp.maximum(before, row_max(x))
            fade = jnp.exp2(before - now)
            total = state[c, 1] * fade
            weights = []
            for j in range(0, x.shape[1], D):
                p = jnp.exp2(x[:, j : j + D] - now)
                if mask is not None:
                    p = jnp.where(mask[:, j : j + D], p, 0.0)
                total = total + p
                weights.append(p.astype(BF16))
            state[c, 0] = now
            state[c, 1] = total
            state[c, 2] = state[c, 2] * fade + jnp.dot(
                jnp.concatenate(weights, 1), values, preferred_element_type=F32
            )

        for s, (flip, rows, extra, first) in enumerate(sources):
            base = (ctx ^ flip) * shard + first
            low = jnp.where(kind == 1, rows, jnp.clip(sink * BLOCK - base, 0, rows))
            high = jnp.clip((total_blocks - window) * BLOCK - base, low, rows)
            span = min(SEGMENT, rows)
            low_end = (low + span - 1) // span

            def step(j, _, s=s, v_at=rows + extra, low=low, high=high, span=span):
                at = pl.multiple_of(j * span, span)
                x = scores_of(q_buf[c], kv[s][pl.ds(at, span), :]) * SCALE
                place = at + lax.broadcasted_iota(jnp.int32, (1, span), 1)
                kept = jnp.broadcast_to((place < low) | (place >= high), x.shape)
                update(x, kv[s][pl.ds(v_at + at, span), :], kept)
                return 0

            lax.fori_loop(0, low_end, step, 0)
            lax.fori_loop(jnp.maximum(high // span, low_end), rows // span, step, 0)
        if with_stretch:
            update(*stretch_parts(c))

    segments = []
    for c in range(n):
        for s, (_, rows, extra, _) in enumerate(sources):
            for at in range(0, rows, SEGMENT):
                segments.append((c, s, at, rows + extra + at, min(SEGMENT, rows - at)))
        if with_stretch:
            segments.append((c, None, 0, 0, wide))

    def all_chunks():
        query = [q_buf[c] for c in range(n)]
        fixed, total, acc = [None] * n, [None] * n, [None] * n
        now = None
        for i in range(len(segments) + 1):
            later = None
            if i < len(segments):
                c, s, at, _, size = segments[i]
                if s is None:
                    later = stretch_parts(c)
                else:
                    later = (scores_of(query[c], kv[s][at : at + size, :]), None, None)
            if i > 0:
                c, s, _, at, size = segments[i - 1]
                x, values, mask = now
                if s is not None:
                    values = kv[s][at : at + size, :]
                    x = x * SCALE
                if i == 1 or segments[i - 2][0] != c:
                    if state_in:
                        fixed[c], total[c], acc[c] = old[c, 0], old[c, 1], old[c, 2]
                    else:
                        fixed[c] = row_max(x[:, :SAMPLE]) + HEADROOM
                weights = []
                for j in range(0, size, D):
                    p = jnp.exp2(x[:, j : j + D] - fixed[c])
                    if mask is not None:
                        p = jnp.where(mask[:, j : j + D], p, 0.0)
                    total[c] = p if total[c] is None else total[c] + p
                    weights.append(p.astype(BF16))
                more = jnp.dot(jnp.concatenate(weights, 1), values, preferred_element_type=F32)
                acc[c] = more if acc[c] is None else acc[c] + more
                if i == len(segments) or segments[i][0] != c:
                    state[c, 0] = fixed[c]
                    state[c, 1] = total[c]
                    state[c, 2] = acc[c]
            now = later
        peak = functools.reduce(jnp.maximum, [jnp.where(t < SAFE, 0.0, 1.0) for t in total])
        return jnp.max(peak) < 0.5

    def every_exact():
        if n == 1:
            exact(0)
        else:

            def step(c, _):
                exact(c)
                return 0

            lax.fori_loop(0, n, step, 0)

    @pl.when(kind == 1)
    def _():
        safe = all_chunks()

        @pl.when(jnp.logical_not(safe))
        def _():
            every_exact()

    @pl.when(kind != 1)
    def _():
        every_exact()

    if emit:
        for c in range(n):
            total = jnp.sum(state[c, 1], axis=1, keepdims=True)
            some = total > 0.0
            total = jnp.where(some, total, 1.0)
            part = state[c, 2] / total
            out[c, :q_rows, :] = part.astype(BF16)
            log_sum = jnp.where(some, state[c, 0] + jnp.log(total) * math.log2(math.e), NEG)
            eye = lax.broadcasted_iota(jnp.int32, (D, D), 0) == lax.broadcasted_iota(
                jnp.int32, (D, D), 1
            )
            lines = []
            for i in range(0, q_rows, D):
                lines.append(
                    jnp.sum(jnp.where(eye, log_sum[i : i + D, :], 0.0), axis=0, keepdims=True)
                )
            lines = jnp.concatenate(lines, 0)
            pieces = []
            for _ in range(3):
                piece = lines.astype(BF16).astype(F32)
                pieces.append(piece)
                lines = lines - piece
            pad = 16 - 3 * (q_rows // D)
            tail = jnp.concatenate(pieces + [jnp.zeros((pad, D), F32)], 0)
            out[c, q_rows:, :] = tail.astype(BF16)


def source_of(ctx, step):
    return (ctx // 8) * 8 + (ctx % 8 - 2 * step + 8) % 8


def attend(tables, queries, steps, sources, shard, state, emit):
    n = len(steps)
    tokens, width = queries[0].shape
    q_rows = tokens * (width // D)
    geom = (
        tuple(steps),
        tuple(source[1:] for source in sources),
        shard,
        lax.axis_size("ctx"),
        state is not None,
        emit,
    )
    shape_state = (n, 3, q_rows, D)
    if emit:
        out_shape = jax.ShapeDtypeStruct((n, q_rows + 16, D), BF16)
        scratch = [pltpu.VMEM((n, q_rows, D), BF16), pltpu.VMEM(shape_state, F32)]
    else:
        out_shape = jax.ShapeDtypeStruct(shape_state, F32)
        scratch = [pltpu.VMEM((n, q_rows, D), BF16)]
    smem = pl.BlockSpec(memory_space=pltpu.SMEM)
    vmem = pl.BlockSpec(memory_space=pltpu.VMEM)
    states = [] if state is None else [state]
    pairs = n * q_rows * sum(source[2] + source[3] for source in sources)
    return pl.pallas_call(
        functools.partial(attend_kernel, geom),
        out_shape=out_shape,
        in_specs=[smem] * 3 + [vmem] * (n + len(sources) + len(states)),
        out_specs=vmem,
        scratch_shapes=scratch,
        compiler_params=pltpu.CompilerParams(vmem_limit_bytes=VMEM_LIMIT),
        cost_estimate=pl.CostEstimate(
            flops=4 * pairs * D,
            bytes_accessed=sum(4 * D * (source[2] + source[3]) for source in sources),
            transcendentals=pairs,
        ),
    )(*tables, *queries, *[source[0] for source in sources], *states)


def combine_kernel(*refs):
    *parts, out = refs
    tokens, width = out.shape
    group = width // D
    q_rows = tokens * group
    for i in range(q_rows // D):
        logs = []
        for part in parts:
            tail = part[q_rows:, :].astype(F32)
            step = q_rows // D
            logs.append(
                tail[i : i + 1] + tail[step + i : step + i + 1] + tail[2 * step + i : 2 * step + i + 1]
            )
        peak = functools.reduce(jnp.maximum, logs)
        weights = [jnp.exp2(x - peak) for x in logs]
        total = functools.reduce(jnp.add, weights)
        acc = jnp.zeros((D, D), F32)
        for part, weight in zip(parts, weights):
            spread = jnp.broadcast_to(weight / total, (D, D)).T
            acc = acc + spread * part[i * D : (i + 1) * D, :].astype(F32)
        for j in range(D // tokens):
            g = i * (D // tokens) + j
            out[:, g * D : (g + 1) * D] = acc[j * tokens : (j + 1) * tokens].astype(BF16)


def combine(parts, tokens, width):
    return pl.pallas_call(
        combine_kernel,
        out_shape=jax.ShapeDtypeStruct((tokens, width), BF16),
        compiler_params=pltpu.CompilerParams(vmem_limit_bytes=16 * 2**20),
    )(*parts)


def flip_perm(count, bits):
    return [(i, i ^ bits) for i in range(count)]


def step_perm(count, step):
    return [(i, (i // 8) * 8 + (i % 8 + 2 * step) % 8) for i in range(count)]


def local(
    queries, stretch_keys, stretch_values, cache_keys, cache_values, head_types, sink_blocks, window_blocks
):
    count = lax.axis_size("ctx")
    tables = (head_types, sink_blocks, window_blocks)
    tokens, width = queries.shape
    shard = cache_keys.shape[0]
    own = stretch_keys.shape[0]

    def send(x, perm):
        return lax.ppermute(x, "ctx", perm)

    cut = CUT
    head_part = jnp.concatenate([cache_keys[:cut], cache_values[:cut]], 0)
    tail_part = jnp.concatenate(
        [cache_keys[cut:], stretch_keys, cache_values[cut:], stretch_values], 0
    )
    messages = [(head_part, cut, 0, 0), (tail_part, shard - cut, own, cut)]
    far = [send(message[0], flip_perm(count, 8)) for message in messages]
    steps = [0, 2, 1, 3]
    chunks = [queries] + [send(queries, step_perm(count, s)) for s in steps[1:]]
    sibling = [send(message[0], flip_perm(count, 1)) for message in messages]

    def call(which, sources, state, emit):
        return attend(
            tables, [chunks[i] for i in which], [steps[i] for i in which], sources, shard, state, emit
        )

    def source(array, flip, i):
        return (array, flip) + messages[i][1:]

    near = [source(messages[i][0], 0, i) for i in (0, 1)]
    near += [source(sibling[i], 1, i) for i in (0, 1)]
    others = [1, 2, 3]
    mine = call([0], near, None, False)
    *later, mine = lax.optimization_barrier((*chunks[1:], mine))
    chunks = [queries, *later]
    rest = call(others, near, None, False)
    far0, rest = lax.optimization_barrier((far[0], rest))
    far0_sibling = send(far0, flip_perm(count, 1))
    first = [source(far0, 8, 0), source(far0_sibling, 9, 0)]
    rest = call(others, first, rest, False)
    far1, rest = lax.optimization_barrier((far[1], rest))
    far1_sibling = send(far1, flip_perm(count, 1))
    second = [source(far1, 8, 1), source(far1_sibling, 9, 1)]
    parts = call(others, second, rest, True)
    back = [send(parts[i], step_perm(count, -steps[i + 1])) for i in range(3)]
    mine = call([0], first + second, mine, True)[0]
    return combine([mine] + back, tokens, width)


def solution(mesh):
    placed = (
        P("ctx", "head"),
        P("ctx", "head"),
        P("ctx", "head"),
        P("ctx", "head"),
        P("ctx", "head"),
        P(),
        P(),
        P(),
    )
    return jax.shard_map(
        local, mesh=mesh, in_specs=placed, out_specs=P("ctx", "head"), check_vma=False
    )
```

```python
import functools
import math

import jax
import jax.numpy as jnp
from jax import lax
from jax.experimental import pallas as pl
from jax.experimental.pallas import tpu as pltpu
from jax.sharding import PartitionSpec as P

D = 128
BLOCK = 128
SCALE = math.log2(math.e) / math.sqrt(D)
NEG = -1e30
HEADROOM = 40.0
SAFE = 2.0**100
SAMPLE = 256
CUT = 1536
SEGMENT = 512
UNROLL = False
VMEM_LIMIT = 32 * 2**20
NT = (((1,), (1,)), ((), ()))
F32 = jnp.float32
BF16 = jnp.bfloat16


def scores_of(query, keys):
    return lax.dot_general(query, keys, NT, preferred_element_type=F32)


def row_max(x):
    peak = functools.reduce(
        jnp.maximum, [x[:, i : i + D] for i in range(0, x.shape[1], D)]
    )
    return jnp.broadcast_to(jnp.max(peak, axis=1, keepdims=True), (x.shape[0], D))


def attend_kernel(geom, *refs):
    steps, sources, shard, ctx_count, state_in, emit = geom
    n, n_src = len(steps), len(sources)
    kinds, sinks, windows = refs[:3]
    q_in = refs[3 : 3 + n]
    kv = refs[3 + n : 3 + n + n_src]
    rest = refs[3 + n + n_src :]
    if state_in:
        old, rest = rest[0], rest[1:]
    out, q_buf = rest[0], rest[1]
    state = rest[2] if emit else out
    group = q_in[0].shape[1] // D
    tokens = q_in[0].shape[0]
    q_rows = group * tokens
    ctx = lax.axis_index("ctx")
    head = lax.axis_index("head")
    kind = kinds[head]
    sink = sinks[head]
    window = windows[head]
    total_blocks = ctx_count * shard // BLOCK

    for c in range(n):
        for g in range(group):
            q_buf[c, g * tokens : (g + 1) * tokens, :] = q_in[c][:, g * D : (g + 1) * D]
    with_stretch = [s for s in range(n_src) if sources[s][2]]
    if with_stretch:
        own = sources[with_stretch[0]][2]
        wide = len(with_stretch) * own
        column = lax.broadcasted_iota(jnp.int32, (q_rows, wide), 1)
        token = lax.broadcasted_iota(jnp.int32, (q_rows, wide), 0) % tokens
        key_pos = jnp.zeros_like(column)
        for i, s in enumerate(with_stretch):
            here = (column >= i * own) & (column < (i + 1) * own)
            key_pos = jnp.where(here, (ctx ^ sources[s][0]) * own + column - i * own, key_pos)

    def stretch_parts(c):
        keys, values = [], []
        for s in with_stretch:
            rows = sources[s][1]
            keys.append(kv[s][rows : rows + own, :])
            values.append(kv[s][2 * rows + own : 2 * rows + 2 * own, :])
        owner = jnp.int32(0)
        for i, step in enumerate(steps):
            owner = jnp.where(c == i, source_of(ctx, step), owner)
        x = scores_of(q_buf[c], jnp.concatenate(keys, 0)) * SCALE
        return x, jnp.concatenate(values, 0), key_pos <= token + owner * tokens

    def exact(c):
        if state_in:
            for i in range(3):
                state[c, i] = old[c, i]
        else:
            state[c, 0] = jnp.full((q_rows, D), NEG, F32)
            state[c, 1] = jnp.zeros((q_rows, D), F32)
            state[c, 2] = jnp.zeros((q_rows, D), F32)

        def update(x, values, mask):
            before = state[c, 0]
            if mask is not None:
                x = jnp.where(mask, x, NEG)
            now = jnp.maximum(before, row_max(x))
            fade = jnp.exp2(before - now)
            total = state[c, 1] * fade
            weights = []
            for j in range(0, x.shape[1], D):
                p = jnp.exp2(x[:, j : j + D] - now)
                if mask is not None:
                    p = jnp.where(mask[:, j : j + D], p, 0.0)
                total = total + p
                weights.append(p.astype(BF16))
            state[c, 0] = now
            state[c, 1] = total
            state[c, 2] = state[c, 2] * fade + jnp.dot(
                jnp.concatenate(weights, 1), values, preferred_element_type=F32
            )

        for s, (flip, rows, extra, first) in enumerate(sources):
            base = (ctx ^ flip) * shard + first
            low = jnp.where(kind == 1, rows, jnp.clip(sink * BLOCK - base, 0, rows))
            high = jnp.clip((total_blocks - window) * BLOCK - base, low, rows)
            span = min(SEGMENT, rows)
            low_end = (low + span - 1) // span
            skip = jnp.maximum(high // span, low_end) - low_end

            def step(j, _, s=s, v_at=rows + extra, low=low, high=high, span=span, low_end=low_end, skip=skip):
                at = pl.multiple_of(jnp.where(j < low_end, j, j + skip) * span, span)
                x = scores_of(q_buf[c], kv[s][pl.ds(at, span), :]) * SCALE
                place = at + lax.broadcasted_iota(jnp.int32, (1, span), 1)
                kept = jnp.broadcast_to((place < low) | (place >= high), x.shape)
                update(x, kv[s][pl.ds(v_at + at, span), :], kept)
                return 0

            lax.fori_loop(0, rows // span - skip, step, 0)
        if with_stretch:
            update(*stretch_parts(c))

    def fixed_stabiliser(chosen):
        segments = []
        for c in range(len(chosen)):
            for s, (_, rows, extra, _) in enumerate(sources):
                for at in range(0, rows, SEGMENT):
                    segments.append((c, s, at, rows + extra + at, min(SEGMENT, rows - at)))
            if with_stretch:
                segments.append((c, None, 0, 0, wide))
        query = [q_buf[c] for c in chosen]
        fixed, total, acc = ([None] * len(chosen) for _ in range(3))
        now = None
        for i in range(len(segments) + 1):
            later = None
            if i < len(segments):
                c, s, at, _, size = segments[i]
                if s is None:
                    later = stretch_parts(chosen[c])
                else:
                    later = (scores_of(query[c], kv[s][at : at + size, :]), None, None)
            if i > 0:
                c, s, _, at, size = segments[i - 1]
                x, values, mask = now
                if s is not None:
                    values = kv[s][at : at + size, :]
                    x = x * SCALE
                if i == 1 or segments[i - 2][0] != c:
                    if state_in:
                        fixed[c], total[c], acc[c] = (old[chosen[c], k] for k in range(3))
                    else:
                        fixed[c] = row_max(x[:, :SAMPLE]) + HEADROOM
                weights = []
                for j in range(0, size, D):
                    p = jnp.exp2(x[:, j : j + D] - fixed[c])
                    if mask is not None:
                        p = jnp.where(mask[:, j : j + D], p, 0.0)
                    total[c] = p if total[c] is None else total[c] + p
                    weights.append(p.astype(BF16))
                more = jnp.dot(jnp.concatenate(weights, 1), values, preferred_element_type=F32)
                acc[c] = more if acc[c] is None else acc[c] + more
                if i == len(segments) or segments[i][0] != c:
                    state[chosen[c], 0] = fixed[c]
                    state[chosen[c], 1] = total[c]
                    state[chosen[c], 2] = acc[c]
            now = later

    def every_exact():
        if n == 1:
            exact(0)
        else:

            def step(c, _):
                exact(c)
                return 0

            lax.fori_loop(0, n, step, 0)

    @pl.when(kind == 1)
    def _():
        if n == 1 or UNROLL:
            fixed_stabiliser(list(range(n)))
        else:

            def one(c, _):
                fixed_stabiliser([c])
                return 0

            lax.fori_loop(0, n, one, 0)
        flags = [jnp.where(state[c, 1] < SAFE, 0.0, 1.0) for c in range(n)]
        safe = jnp.max(functools.reduce(jnp.maximum, flags)) < 0.5

        @pl.when(jnp.logical_not(safe))
        def _():
            every_exact()

    @pl.when(kind != 1)
    def _():
        every_exact()

    if emit:

        def hand_out(c, _):
            total = jnp.sum(state[c, 1], axis=1, keepdims=True)
            some = total > 0.0
            total = jnp.where(some, total, 1.0)
            part = state[c, 2] / total
            out[c, :q_rows, :] = part.astype(BF16)
            log_sum = jnp.where(some, state[c, 0] + jnp.log(total) * math.log2(math.e), NEG)
            eye = lax.broadcasted_iota(jnp.int32, (D, D), 0) == lax.broadcasted_iota(
                jnp.int32, (D, D), 1
            )
            lines = []
            for i in range(0, q_rows, D):
                lines.append(
                    jnp.sum(jnp.where(eye, log_sum[i : i + D, :], 0.0), axis=0, keepdims=True)
                )
            lines = jnp.concatenate(lines, 0)
            pieces = []
            for _ in range(3):
                piece = lines.astype(BF16).astype(F32)
                pieces.append(piece)
                lines = lines - piece
            pad = 16 - 3 * (q_rows // D)
            tail = jnp.concatenate(pieces + [jnp.zeros((pad, D), F32)], 0)
            out[c, q_rows:, :] = tail.astype(BF16)
            return 0

        if n == 1:
            hand_out(0, 0)
        else:
            lax.fori_loop(0, n, hand_out, 0)


def source_of(ctx, step):
    return (ctx // 8) * 8 + (ctx % 8 - 2 * step + 8) % 8


def attend(tables, queries, steps, sources, shard, state, emit):
    n = len(steps)
    tokens, width = queries[0].shape
    q_rows = tokens * (width // D)
    geom = (
        tuple(steps),
        tuple(source[1:] for source in sources),
        shard,
        lax.axis_size("ctx"),
        state is not None,
        emit,
    )
    shape_state = (n, 3, q_rows, D)
    if emit:
        out_shape = jax.ShapeDtypeStruct((n, q_rows + 16, D), BF16)
        scratch = [pltpu.VMEM((n, q_rows, D), BF16), pltpu.VMEM(shape_state, F32)]
    else:
        out_shape = jax.ShapeDtypeStruct(shape_state, F32)
        scratch = [pltpu.VMEM((n, q_rows, D), BF16)]
    smem = pl.BlockSpec(memory_space=pltpu.SMEM)
    vmem = pl.BlockSpec(memory_space=pltpu.VMEM)
    states = [] if state is None else [state]
    pairs = n * q_rows * sum(source[2] + source[3] for source in sources)
    return pl.pallas_call(
        functools.partial(attend_kernel, geom),
        out_shape=out_shape,
        in_specs=[smem] * 3 + [vmem] * (n + len(sources) + len(states)),
        out_specs=vmem,
        scratch_shapes=scratch,
        compiler_params=pltpu.CompilerParams(vmem_limit_bytes=VMEM_LIMIT),
        cost_estimate=pl.CostEstimate(
            flops=4 * pairs * D,
            bytes_accessed=sum(4 * D * (source[2] + source[3]) for source in sources),
            transcendentals=pairs,
        ),
    )(*tables, *queries, *[source[0] for source in sources], *states)


def combine_kernel(*refs):
    *parts, out = refs
    tokens, width = out.shape
    group = width // D
    q_rows = tokens * group
    for i in range(q_rows // D):
        logs = []
        for part in parts:
            tail = part[q_rows:, :].astype(F32)
            step = q_rows // D
            logs.append(
                tail[i : i + 1] + tail[step + i : step + i + 1] + tail[2 * step + i : 2 * step + i + 1]
            )
        peak = functools.reduce(jnp.maximum, logs)
        weights = [jnp.exp2(x - peak) for x in logs]
        total = functools.reduce(jnp.add, weights)
        acc = jnp.zeros((D, D), F32)
        for part, weight in zip(parts, weights):
            spread = jnp.broadcast_to(weight / total, (D, D)).T
            acc = acc + spread * part[i * D : (i + 1) * D, :].astype(F32)
        for j in range(D // tokens):
            g = i * (D // tokens) + j
            out[:, g * D : (g + 1) * D] = acc[j * tokens : (j + 1) * tokens].astype(BF16)


def combine(parts, tokens, width):
    return pl.pallas_call(
        combine_kernel,
        out_shape=jax.ShapeDtypeStruct((tokens, width), BF16),
        compiler_params=pltpu.CompilerParams(vmem_limit_bytes=16 * 2**20),
    )(*parts)


def flip_perm(count, bits):
    return [(i, i ^ bits) for i in range(count)]


def step_perm(count, step):
    return [(i, (i // 8) * 8 + (i % 8 + 2 * step) % 8) for i in range(count)]


def local(
    queries, stretch_keys, stretch_values, cache_keys, cache_values, head_types, sink_blocks, window_blocks
):
    count = lax.axis_size("ctx")
    tables = (head_types, sink_blocks, window_blocks)
    tokens, width = queries.shape
    shard = cache_keys.shape[0]
    own = stretch_keys.shape[0]

    def send(x, perm):
        return lax.ppermute(x, "ctx", perm)

    cut = CUT
    head_part = jnp.concatenate([cache_keys[:cut], cache_values[:cut]], 0)
    tail_part = jnp.concatenate(
        [cache_keys[cut:], stretch_keys, cache_values[cut:], stretch_values], 0
    )
    messages = [(head_part, cut, 0, 0), (tail_part, shard - cut, own, cut)]
    far = [send(message[0], flip_perm(count, 8)) for message in messages]
    steps = [0, 2, 1, 3]
    chunks = [queries] + [send(queries, step_perm(count, s)) for s in steps[1:]]
    sibling = [send(message[0], flip_perm(count, 1)) for message in messages]

    def call(which, sources, state, emit):
        return attend(
            tables, [chunks[i] for i in which], [steps[i] for i in which], sources, shard, state, emit
        )

    def source(array, flip, i):
        return (array, flip) + messages[i][1:]

    near = [source(messages[i][0], 0, i) for i in (0, 1)]
    near += [source(sibling[i], 1, i) for i in (0, 1)]
    others = [1, 2, 3]
    mine = call([0], near, None, False)
    *later, mine = lax.optimization_barrier((*chunks[1:], mine))
    chunks = [queries, *later]
    rest = call(others, near, None, False)
    far0, rest = lax.optimization_barrier((far[0], rest))
    far0_sibling = send(far0, flip_perm(count, 1))
    first = [source(far0, 8, 0), source(far0_sibling, 9, 0)]
    rest = call(others, first, rest, False)
    far1, rest = lax.optimization_barrier((far[1], rest))
    far1_sibling = send(far1, flip_perm(count, 1))
    second = [source(far1, 8, 1), source(far1_sibling, 9, 1)]
    parts = call(others, second, rest, True)
    back = [send(parts[i], step_perm(count, -steps[i + 1])) for i in range(3)]
    mine = call([0], first + second, mine, True)[0]
    return combine([mine] + back, tokens, width)


def solution(mesh):
    placed = (
        P("ctx", "head"),
        P("ctx", "head"),
        P("ctx", "head"),
        P("ctx", "head"),
        P("ctx", "head"),
        P(),
        P(),
        P(),
    )
    return jax.shard_map(
        local, mesh=mesh, in_specs=placed, out_specs=P("ctx", "head"), check_vma=False
    )
```

```python
import functools
import math

import jax
import jax.numpy as jnp
from jax import lax
from jax.experimental import pallas as pl
from jax.experimental.pallas import tpu as pltpu
from jax.sharding import PartitionSpec as P

D = 128
BLOCK = 128
SCALE = math.log2(math.e) / math.sqrt(D)
NEG = -1e30
HEADROOM = 40.0
SAFE = 2.0**100
SAMPLE = 256
CUT = 1536
SEGMENT = 512
UNROLL = False
VMEM_LIMIT = 32 * 2**20
NT = (((1,), (1,)), ((), ()))
F32 = jnp.float32
BF16 = jnp.bfloat16


def scores_of(query, keys):
    return lax.dot_general(query, keys, NT, preferred_element_type=F32)


def row_max(x):
    peak = functools.reduce(
        jnp.maximum, [x[:, i : i + D] for i in range(0, x.shape[1], D)]
    )
    return jnp.broadcast_to(jnp.max(peak, axis=1, keepdims=True), (x.shape[0], D))


def attend_kernel(geom, *refs):
    steps, sources, shard, ctx_count, state_in, emit = geom
    n, n_src = len(steps), len(sources)
    kinds, sinks, windows = refs[:3]
    q_in = refs[3 : 3 + n]
    kv = refs[3 + n : 3 + n + n_src]
    rest = refs[3 + n + n_src :]
    old, rest = rest[: len(state_in)], rest[len(state_in) :]
    out, q_buf = rest[0], rest[1]
    state = rest[2] if emit else out
    group = q_in[0].shape[1] // D
    tokens = q_in[0].shape[0]
    q_rows = group * tokens
    ctx = lax.axis_index("ctx")
    head = lax.axis_index("head")
    kind = kinds[head]
    sink = sinks[head]
    window = windows[head]
    total_blocks = ctx_count * shard // BLOCK

    for c in range(n):
        for g in range(group):
            q_buf[c, g * tokens : (g + 1) * tokens, :] = q_in[c][:, g * D : (g + 1) * D]
    with_stretch = [s for s in range(n_src) if sources[s][2]]
    if with_stretch:
        own = sources[with_stretch[0]][2]
        wide = len(with_stretch) * own
        column = lax.broadcasted_iota(jnp.int32, (q_rows, wide), 1)
        token = lax.broadcasted_iota(jnp.int32, (q_rows, wide), 0) % tokens
        key_pos = jnp.zeros_like(column)
        for i, s in enumerate(with_stretch):
            here = (column >= i * own) & (column < (i + 1) * own)
            key_pos = jnp.where(here, (ctx ^ sources[s][0]) * own + column - i * own, key_pos)

    def stretch_parts(c):
        keys, values = [], []
        for s in with_stretch:
            rows = sources[s][1]
            keys.append(kv[s][rows : rows + own, :])
            values.append(kv[s][2 * rows + own : 2 * rows + 2 * own, :])
        owner = jnp.int32(0)
        for i, step in enumerate(steps):
            owner = jnp.where(c == i, source_of(ctx, step), owner)
        x = scores_of(q_buf[c], jnp.concatenate(keys, 0)) * SCALE
        return x, jnp.concatenate(values, 0), key_pos <= token + owner * tokens

    places = [(ref, j) for ref, size in zip(old, state_in) for j in range(size)]

    def restore():
        for c in range(n):
            if state_in:
                ref, j = places[c]
                for i in range(3):
                    state[c, i] = ref[j, i]
            else:
                state[c, 0] = jnp.full((q_rows, D), NEG, F32)
                for i in (1, 2):
                    state[c, i] = jnp.zeros((q_rows, D), F32)

    begin = old[0] if len(state_in) == 1 else state

    def exact(c):
        def update(x, values, mask):
            before = state[c, 0]
            if mask is not None:
                x = jnp.where(mask, x, NEG)
            now = jnp.maximum(before, row_max(x))
            fade = jnp.exp2(before - now)
            total = state[c, 1] * fade
            weights = []
            for j in range(0, x.shape[1], D):
                p = jnp.exp2(x[:, j : j + D] - now)
                if mask is not None:
                    p = jnp.where(mask[:, j : j + D], p, 0.0)
                total = total + p
                weights.append(p.astype(BF16))
            state[c, 0] = now
            state[c, 1] = total
            state[c, 2] = state[c, 2] * fade + jnp.dot(
                jnp.concatenate(weights, 1), values, preferred_element_type=F32
            )

        for s, (flip, rows, extra, first) in enumerate(sources):
            base = (ctx ^ flip) * shard + first
            low = jnp.where(kind == 1, rows, jnp.clip(sink * BLOCK - base, 0, rows))
            high = jnp.clip((total_blocks - window) * BLOCK - base, low, rows)
            span = min(SEGMENT, rows)
            low_end = (low + span - 1) // span
            skip = jnp.maximum(high // span, low_end) - low_end

            def step(j, _, s=s, v_at=rows + extra, low=low, high=high, span=span, low_end=low_end, skip=skip):
                at = pl.multiple_of(jnp.where(j < low_end, j, j + skip) * span, span)
                x = scores_of(q_buf[c], kv[s][pl.ds(at, span), :]) * SCALE
                place = at + lax.broadcasted_iota(jnp.int32, (1, span), 1)
                kept = jnp.broadcast_to((place < low) | (place >= high), x.shape)
                update(x, kv[s][pl.ds(v_at + at, span), :], kept)
                return 0

            lax.fori_loop(0, rows // span - skip, step, 0)
        if with_stretch:
            update(*stretch_parts(c))

    def fixed_stabiliser(chosen):
        segments = []
        for c in range(len(chosen)):
            for s, (_, rows, extra, _) in enumerate(sources):
                for at in range(0, rows, SEGMENT):
                    segments.append((c, s, at, rows + extra + at, min(SEGMENT, rows - at)))
            if with_stretch:
                segments.append((c, None, 0, 0, wide))
        query = [q_buf[c] for c in chosen]
        fixed, total, acc = ([None] * len(chosen) for _ in range(3))
        now = None
        for i in range(len(segments) + 1):
            later = None
            if i < len(segments):
                c, s, at, _, size = segments[i]
                if s is None:
                    later = stretch_parts(chosen[c])
                else:
                    later = (scores_of(query[c], kv[s][at : at + size, :]), None, None)
            if i > 0:
                c, s, _, at, size = segments[i - 1]
                x, values, mask = now
                if s is not None:
                    values = kv[s][at : at + size, :]
                    x = x * SCALE
                if i == 1 or segments[i - 2][0] != c:
                    if state_in:
                        fixed[c], total[c], acc[c] = (begin[chosen[c], k] for k in range(3))
                    else:
                        fixed[c] = row_max(x[:, :SAMPLE]) + HEADROOM
                weights = []
                for j in range(0, size, D):
                    p = jnp.exp2(x[:, j : j + D] - fixed[c])
                    if mask is not None:
                        p = jnp.where(mask[:, j : j + D], p, 0.0)
                    total[c] = p if total[c] is None else total[c] + p
                    weights.append(p.astype(BF16))
                more = jnp.dot(jnp.concatenate(weights, 1), values, preferred_element_type=F32)
                acc[c] = more if acc[c] is None else acc[c] + more
                if i == len(segments) or segments[i][0] != c:
                    state[chosen[c], 0] = fixed[c]
                    state[chosen[c], 1] = total[c]
                    state[chosen[c], 2] = acc[c]
            now = later

    def every_exact():
        if n == 1:
            exact(0)
        else:

            def step(c, _):
                exact(c)
                return 0

            lax.fori_loop(0, n, step, 0)

    def quick():
        if len(state_in) > 1:
            restore()
        if n == 1 or UNROLL:
            fixed_stabiliser(list(range(n)))
        else:

            def one(c, _):
                fixed_stabiliser([c])
                return 0

            lax.fori_loop(0, n, one, 0)
        flags = [jnp.where(state[c, 1] < SAFE, 0.0, 1.0) for c in range(n)]
        return jnp.where(jnp.max(functools.reduce(jnp.maximum, flags)) < 0.5, 0, 1)

    left_over = lax.cond(kind == 1, quick, lambda: jnp.int32(1))

    @pl.when(left_over == 1)
    def _():
        restore()
        every_exact()

    if emit:

        def hand_out(c, _):
            total = jnp.sum(state[c, 1], axis=1, keepdims=True)
            some = total > 0.0
            total = jnp.where(some, total, 1.0)
            part = state[c, 2] / total
            out[c, :q_rows, :] = part.astype(BF16)
            log_sum = jnp.where(some, state[c, 0] + jnp.log(total) * math.log2(math.e), NEG)
            eye = lax.broadcasted_iota(jnp.int32, (D, D), 0) == lax.broadcasted_iota(
                jnp.int32, (D, D), 1
            )
            lines = []
            for i in range(0, q_rows, D):
                lines.append(
                    jnp.sum(jnp.where(eye, log_sum[i : i + D, :], 0.0), axis=0, keepdims=True)
                )
            lines = jnp.concatenate(lines, 0)
            pieces = []
            for _ in range(3):
                piece = lines.astype(BF16).astype(F32)
                pieces.append(piece)
                lines = lines - piece
            pad = 16 - 3 * (q_rows // D)
            tail = jnp.concatenate(pieces + [jnp.zeros((pad, D), F32)], 0)
            out[c, q_rows:, :] = tail.astype(BF16)
            return 0

        if n == 1:
            hand_out(0, 0)
        else:
            lax.fori_loop(0, n, hand_out, 0)


def source_of(ctx, step):
    return (ctx // 8) * 8 + (ctx % 8 - 2 * step + 8) % 8


def attend(tables, queries, steps, sources, shard, states, emit):
    n = len(steps)
    tokens, width = queries[0].shape
    q_rows = tokens * (width // D)
    geom = (
        tuple(steps),
        tuple(source[1:] for source in sources),
        shard,
        lax.axis_size("ctx"),
        tuple(array.shape[0] for array in states),
        emit,
    )
    shape_state = (n, 3, q_rows, D)
    if emit:
        out_shape = jax.ShapeDtypeStruct((n, q_rows + 16, D), BF16)
        scratch = [pltpu.VMEM((n, q_rows, D), BF16), pltpu.VMEM(shape_state, F32)]
    else:
        out_shape = jax.ShapeDtypeStruct(shape_state, F32)
        scratch = [pltpu.VMEM((n, q_rows, D), BF16)]
    smem = pl.BlockSpec(memory_space=pltpu.SMEM)
    vmem = pl.BlockSpec(memory_space=pltpu.VMEM)
    pairs = n * q_rows * sum(source[2] + source[3] for source in sources)
    return pl.pallas_call(
        functools.partial(attend_kernel, geom),
        out_shape=out_shape,
        in_specs=[smem] * 3 + [vmem] * (n + len(sources) + len(states)),
        out_specs=vmem,
        scratch_shapes=scratch,
        compiler_params=pltpu.CompilerParams(vmem_limit_bytes=VMEM_LIMIT),
        cost_estimate=pl.CostEstimate(
            flops=4 * pairs * D,
            bytes_accessed=sum(4 * D * (source[2] + source[3]) for source in sources),
            transcendentals=pairs,
        ),
    )(*tables, *queries, *[source[0] for source in sources], *states)


def combine_kernel(*refs):
    *parts, out = refs
    tokens, width = out.shape
    group = width // D
    q_rows = tokens * group
    for i in range(q_rows // D):
        logs = []
        for part in parts:
            tail = part[q_rows:, :].astype(F32)
            step = q_rows // D
            logs.append(
                tail[i : i + 1] + tail[step + i : step + i + 1] + tail[2 * step + i : 2 * step + i + 1]
            )
        peak = functools.reduce(jnp.maximum, logs)
        weights = [jnp.exp2(x - peak) for x in logs]
        total = functools.reduce(jnp.add, weights)
        acc = jnp.zeros((D, D), F32)
        for part, weight in zip(parts, weights):
            spread = jnp.broadcast_to(weight / total, (D, D)).T
            acc = acc + spread * part[i * D : (i + 1) * D, :].astype(F32)
        for j in range(D // tokens):
            g = i * (D // tokens) + j
            out[:, g * D : (g + 1) * D] = acc[j * tokens : (j + 1) * tokens].astype(BF16)


def combine(parts, tokens, width):
    return pl.pallas_call(
        combine_kernel,
        out_shape=jax.ShapeDtypeStruct((tokens, width), BF16),
        compiler_params=pltpu.CompilerParams(vmem_limit_bytes=16 * 2**20),
    )(*parts)


def flip_perm(count, bits):
    return [(i, i ^ bits) for i in range(count)]


def step_perm(count, step):
    return [(i, (i // 8) * 8 + (i % 8 + 2 * step) % 8) for i in range(count)]


def local(
    queries, stretch_keys, stretch_values, cache_keys, cache_values, head_types, sink_blocks, window_blocks
):
    count = lax.axis_size("ctx")
    tables = (head_types, sink_blocks, window_blocks)
    tokens, width = queries.shape
    shard = cache_keys.shape[0]
    own = stretch_keys.shape[0]

    def send(x, perm):
        return lax.ppermute(x, "ctx", perm)

    cut = CUT
    head_part = jnp.concatenate([cache_keys[:cut], cache_values[:cut]], 0)
    tail_part = jnp.concatenate(
        [cache_keys[cut:], stretch_keys, cache_values[cut:], stretch_values], 0
    )
    messages = [(head_part, cut, 0, 0), (tail_part, shard - cut, own, cut)]
    far = [send(message[0], flip_perm(count, 8)) for message in messages]
    steps = [0, 3, 1, 2]
    chunks = [queries] + [send(queries, step_perm(count, s)) for s in steps[1:]]
    sibling = [send(message[0], flip_perm(count, 1)) for message in messages]

    def call(which, sources, states, emit):
        return attend(
            tables, [chunks[i] for i in which], [steps[i] for i in which], sources, shard, states, emit
        )

    def source(array, flip, i):
        return (array, flip) + messages[i][1:]

    near = [source(messages[i][0], 0, i) for i in (0, 1)]
    near += [source(sibling[i], 1, i) for i in (0, 1)]
    others = [1, 2, 3]
    mine = call([0], near, [], False)
    chunks[1], mine = lax.optimization_barrier((chunks[1], mine))
    left = call([1], near, [], False)
    chunks[2], chunks[3], left = lax.optimization_barrier((*chunks[2:], left))
    right = call([2, 3], near, [], False)
    far0, right = lax.optimization_barrier((far[0], right))
    far0_sibling = send(far0, flip_perm(count, 1))
    first = [source(far0, 8, 0), source(far0_sibling, 9, 0)]
    rest = call(others, first, [left, right], False)
    far1, rest = lax.optimization_barrier((far[1], rest))
    far1_sibling = send(far1, flip_perm(count, 1))
    second = [source(far1, 8, 1), source(far1_sibling, 9, 1)]
    parts = call(others, second, [rest], True)
    back = [send(parts[i], step_perm(count, -steps[i + 1])) for i in range(3)]
    mine = call([0], first + second, [mine], True)[0]
    return combine([mine] + back, tokens, width)


def solution(mesh):
    placed = (
        P("ctx", "head"),
        P("ctx", "head"),
        P("ctx", "head"),
        P("ctx", "head"),
        P("ctx", "head"),
        P(),
        P(),
        P(),
    )
    return jax.shard_map(
        local, mesh=mesh, in_specs=placed, out_specs=P("ctx", "head"), check_vma=False
    )
```

```python
import functools
import math

import jax
import jax.numpy as jnp
from jax import lax
from jax.experimental import pallas as pl
from jax.experimental.pallas import tpu as pltpu
from jax.sharding import PartitionSpec as P

D = 128
BLOCK = 128
SCALE = math.log2(math.e) / math.sqrt(D)
NEG = -1e30
HEADROOM = 40.0
SAFE = 2.0**100
SAMPLE = 256
CUT = 1536
SEGMENT = 512
UNROLL = True
VMEM_LIMIT = 32 * 2**20
NT = (((1,), (1,)), ((), ()))
F32 = jnp.float32
BF16 = jnp.bfloat16


def scores_of(query, keys):
    return lax.dot_general(query, keys, NT, preferred_element_type=F32)


def row_max(x):
    peak = functools.reduce(
        jnp.maximum, [x[:, i : i + D] for i in range(0, x.shape[1], D)]
    )
    return jnp.broadcast_to(jnp.max(peak, axis=1, keepdims=True), (x.shape[0], D))


def attend_kernel(geom, *refs):
    steps, sources, shard, ctx_count, state_in, emit = geom
    n, n_src = len(steps), len(sources)
    kinds, sinks, windows = refs[:3]
    q_in = refs[3 : 3 + n]
    kv = refs[3 + n : 3 + n + n_src]
    rest = refs[3 + n + n_src :]
    old, rest = rest[: len(state_in)], rest[len(state_in) :]
    out, q_buf = rest[0], rest[1]
    state = rest[2] if emit else out
    group = q_in[0].shape[1] // D
    tokens = q_in[0].shape[0]
    q_rows = group * tokens
    ctx = lax.axis_index("ctx")
    head = lax.axis_index("head")
    kind = kinds[head]
    sink = sinks[head]
    window = windows[head]
    total_blocks = ctx_count * shard // BLOCK

    for c in range(n):
        for g in range(group):
            q_buf[c, g * tokens : (g + 1) * tokens, :] = q_in[c][:, g * D : (g + 1) * D]
    with_stretch = [s for s in range(n_src) if sources[s][2]]
    if with_stretch:
        own = sources[with_stretch[0]][2]
        wide = len(with_stretch) * own
        column = lax.broadcasted_iota(jnp.int32, (q_rows, wide), 1)
        token = lax.broadcasted_iota(jnp.int32, (q_rows, wide), 0) % tokens
        key_pos = jnp.zeros_like(column)
        for i, s in enumerate(with_stretch):
            here = (column >= i * own) & (column < (i + 1) * own)
            key_pos = jnp.where(here, (ctx ^ sources[s][0]) * own + column - i * own, key_pos)

    def stretch_parts(c):
        keys, values = [], []
        for s in with_stretch:
            rows = sources[s][1]
            keys.append(kv[s][rows : rows + own, :])
            values.append(kv[s][2 * rows + own : 2 * rows + 2 * own, :])
        owner = jnp.int32(0)
        for i, step in enumerate(steps):
            owner = jnp.where(c == i, source_of(ctx, step), owner)
        x = scores_of(q_buf[c], jnp.concatenate(keys, 0)) * SCALE
        return x, jnp.concatenate(values, 0), key_pos <= token + owner * tokens

    places = [(ref, j) for ref, size in zip(old, state_in) for j in range(size)]

    def restore():
        for c in range(n):
            if state_in:
                ref, j = places[c]
                for i in range(3):
                    state[c, i] = ref[j, i]
            else:
                state[c, 0] = jnp.full((q_rows, D), NEG, F32)
                for i in (1, 2):
                    state[c, i] = jnp.zeros((q_rows, D), F32)

    begin = old[0] if len(state_in) == 1 else state

    def exact(c):
        def update(x, values, mask):
            before = state[c, 0]
            if mask is not None:
                x = jnp.where(mask, x, NEG)
            now = jnp.maximum(before, row_max(x))
            fade = jnp.exp2(before - now)
            total = state[c, 1] * fade
            weights = []
            for j in range(0, x.shape[1], D):
                p = jnp.exp2(x[:, j : j + D] - now)
                if mask is not None:
                    p = jnp.where(mask[:, j : j + D], p, 0.0)
                total = total + p
                weights.append(p.astype(BF16))
            state[c, 0] = now
            state[c, 1] = total
            state[c, 2] = state[c, 2] * fade + jnp.dot(
                jnp.concatenate(weights, 1), values, preferred_element_type=F32
            )

        for s, (flip, rows, extra, first) in enumerate(sources):
            base = (ctx ^ flip) * shard + first
            low = jnp.where(kind == 1, rows, jnp.clip(sink * BLOCK - base, 0, rows))
            high = jnp.clip((total_blocks - window) * BLOCK - base, low, rows)
            span = min(SEGMENT, rows)
            low_end = (low + span - 1) // span
            skip = jnp.maximum(high // span, low_end) - low_end

            def step(j, _, s=s, v_at=rows + extra, low=low, high=high, span=span, low_end=low_end, skip=skip):
                at = pl.multiple_of(jnp.where(j < low_end, j, j + skip) * span, span)
                x = scores_of(q_buf[c], kv[s][pl.ds(at, span), :]) * SCALE
                place = at + lax.broadcasted_iota(jnp.int32, (1, span), 1)
                kept = jnp.broadcast_to((place < low) | (place >= high), x.shape)
                update(x, kv[s][pl.ds(v_at + at, span), :], kept)
                return 0

            lax.fori_loop(0, rows // span - skip, step, 0)
        if with_stretch:
            update(*stretch_parts(c))

    def fixed_stabiliser(chosen):
        segments = []
        for c in range(len(chosen)):
            for s, (_, rows, extra, _) in enumerate(sources):
                for at in range(0, rows, SEGMENT):
                    segments.append((c, s, at, rows + extra + at, min(SEGMENT, rows - at)))
            if with_stretch:
                segments.append((c, None, 0, 0, wide))
        query = [q_buf[c] for c in chosen]
        fixed, total, acc = ([None] * len(chosen) for _ in range(3))
        now = None
        for i in range(len(segments) + 1):
            later = None
            if i < len(segments):
                c, s, at, _, size = segments[i]
                if s is None:
                    later = stretch_parts(chosen[c])
                else:
                    later = (scores_of(query[c], kv[s][at : at + size, :]), None, None)
            if i > 0:
                c, s, _, at, size = segments[i - 1]
                x, values, mask = now
                if s is not None:
                    values = kv[s][at : at + size, :]
                    x = x * SCALE
                if i == 1 or segments[i - 2][0] != c:
                    if state_in:
                        fixed[c], total[c], acc[c] = (begin[chosen[c], k] for k in range(3))
                    else:
                        fixed[c] = row_max(x[:, :SAMPLE]) + HEADROOM
                weights = []
                for j in range(0, size, D):
                    p = jnp.exp2(x[:, j : j + D] - fixed[c])
                    if mask is not None:
                        p = jnp.where(mask[:, j : j + D], p, 0.0)
                    total[c] = p if total[c] is None else total[c] + p
                    weights.append(p.astype(BF16))
                more = jnp.dot(jnp.concatenate(weights, 1), values, preferred_element_type=F32)
                acc[c] = more if acc[c] is None else acc[c] + more
                if i == len(segments) or segments[i][0] != c:
                    state[chosen[c], 0] = fixed[c]
                    state[chosen[c], 1] = total[c]
                    state[chosen[c], 2] = acc[c]
            now = later

    def every_exact():
        if n == 1:
            exact(0)
        else:

            def step(c, _):
                exact(c)
                return 0

            lax.fori_loop(0, n, step, 0)

    def quick():
        if len(state_in) > 1:
            restore()
        if n < 3 or (emit and UNROLL):
            fixed_stabiliser(list(range(n)))
        else:

            def one(c, _):
                fixed_stabiliser([c])
                return 0

            lax.fori_loop(0, n, one, 0)
        flags = [jnp.where(state[c, 1] < SAFE, 0.0, 1.0) for c in range(n)]
        return jnp.where(jnp.max(functools.reduce(jnp.maximum, flags)) < 0.5, 0, 1)

    left_over = lax.cond(kind == 1, quick, lambda: jnp.int32(1))

    @pl.when(left_over == 1)
    def _():
        restore()
        every_exact()

    if emit:

        def hand_out(c, _):
            total = jnp.sum(state[c, 1], axis=1, keepdims=True)
            some = total > 0.0
            total = jnp.where(some, total, 1.0)
            part = state[c, 2] / total
            out[c, :q_rows, :] = part.astype(BF16)
            log_sum = jnp.where(some, state[c, 0] + jnp.log(total) * math.log2(math.e), NEG)
            eye = lax.broadcasted_iota(jnp.int32, (D, D), 0) == lax.broadcasted_iota(
                jnp.int32, (D, D), 1
            )
            lines = []
            for i in range(0, q_rows, D):
                lines.append(
                    jnp.sum(jnp.where(eye, log_sum[i : i + D, :], 0.0), axis=0, keepdims=True)
                )
            lines = jnp.concatenate(lines, 0)
            pieces = []
            for _ in range(3):
                piece = lines.astype(BF16).astype(F32)
                pieces.append(piece)
                lines = lines - piece
            pad = 16 - 3 * (q_rows // D)
            tail = jnp.concatenate(pieces + [jnp.zeros((pad, D), F32)], 0)
            out[c, q_rows:, :] = tail.astype(BF16)
            return 0

        if n == 1:
            hand_out(0, 0)
        else:
            lax.fori_loop(0, n, hand_out, 0)


def source_of(ctx, step):
    return (ctx // 8) * 8 + (ctx % 8 - 2 * step + 8) % 8


def attend(tables, queries, steps, sources, shard, states, emit):
    n = len(steps)
    tokens, width = queries[0].shape
    q_rows = tokens * (width // D)
    geom = (
        tuple(steps),
        tuple(source[1:] for source in sources),
        shard,
        lax.axis_size("ctx"),
        tuple(array.shape[0] for array in states),
        emit,
    )
    shape_state = (n, 3, q_rows, D)
    if emit:
        out_shape = jax.ShapeDtypeStruct((n, q_rows + 16, D), BF16)
        scratch = [pltpu.VMEM((n, q_rows, D), BF16), pltpu.VMEM(shape_state, F32)]
    else:
        out_shape = jax.ShapeDtypeStruct(shape_state, F32)
        scratch = [pltpu.VMEM((n, q_rows, D), BF16)]
    smem = pl.BlockSpec(memory_space=pltpu.SMEM)
    vmem = pl.BlockSpec(memory_space=pltpu.VMEM)
    pairs = n * q_rows * sum(source[2] + source[3] for source in sources)
    return pl.pallas_call(
        functools.partial(attend_kernel, geom),
        out_shape=out_shape,
        in_specs=[smem] * 3 + [vmem] * (n + len(sources) + len(states)),
        out_specs=vmem,
        scratch_shapes=scratch,
        compiler_params=pltpu.CompilerParams(vmem_limit_bytes=VMEM_LIMIT),
        cost_estimate=pl.CostEstimate(
            flops=4 * pairs * D,
            bytes_accessed=sum(4 * D * (source[2] + source[3]) for source in sources),
            transcendentals=pairs,
        ),
    )(*tables, *queries, *[source[0] for source in sources], *states)


def combine_kernel(*refs):
    *parts, out = refs
    tokens, width = out.shape
    group = width // D
    q_rows = tokens * group
    for i in range(q_rows // D):
        logs = []
        for part in parts:
            tail = part[q_rows:, :].astype(F32)
            step = q_rows // D
            logs.append(
                tail[i : i + 1] + tail[step + i : step + i + 1] + tail[2 * step + i : 2 * step + i + 1]
            )
        peak = functools.reduce(jnp.maximum, logs)
        weights = [jnp.exp2(x - peak) for x in logs]
        total = functools.reduce(jnp.add, weights)
        acc = jnp.zeros((D, D), F32)
        for part, weight in zip(parts, weights):
            spread = jnp.broadcast_to(weight / total, (D, D)).T
            acc = acc + spread * part[i * D : (i + 1) * D, :].astype(F32)
        for j in range(D // tokens):
            g = i * (D // tokens) + j
            out[:, g * D : (g + 1) * D] = acc[j * tokens : (j + 1) * tokens].astype(BF16)


def combine(parts, tokens, width):
    return pl.pallas_call(
        combine_kernel,
        out_shape=jax.ShapeDtypeStruct((tokens, width), BF16),
        compiler_params=pltpu.CompilerParams(vmem_limit_bytes=16 * 2**20),
    )(*parts)


def flip_perm(count, bits):
    return [(i, i ^ bits) for i in range(count)]


def step_perm(count, step):
    return [(i, (i // 8) * 8 + (i % 8 + 2 * step) % 8) for i in range(count)]


def local(
    queries, stretch_keys, stretch_values, cache_keys, cache_values, head_types, sink_blocks, window_blocks
):
    count = lax.axis_size("ctx")
    tables = (head_types, sink_blocks, window_blocks)
    tokens, width = queries.shape
    shard = cache_keys.shape[0]
    own = stretch_keys.shape[0]

    def send(x, perm):
        return lax.ppermute(x, "ctx", perm)

    cut = CUT
    head_part = jnp.concatenate([cache_keys[:cut], cache_values[:cut]], 0)
    tail_part = jnp.concatenate(
        [cache_keys[cut:], stretch_keys, cache_values[cut:], stretch_values], 0
    )
    messages = [(head_part, cut, 0, 0), (tail_part, shard - cut, own, cut)]
    far0 = send(messages[0][0], flip_perm(count, 8))
    steps = [0, 3, 1, 2]
    chunks = [queries] + [send(queries, step_perm(count, s)) for s in steps[1:]]
    sibling = [send(message[0], flip_perm(count, 1)) for message in messages]

    def call(which, sources, states, emit):
        return attend(
            tables, [chunks[i] for i in which], [steps[i] for i in which], sources, shard, states, emit
        )

    def source(array, flip, i):
        return (array, flip) + messages[i][1:]

    near = [source(messages[i][0], 0, i) for i in (0, 1)]
    near += [source(sibling[i], 1, i) for i in (0, 1)]
    others = [1, 2, 3]
    mine = call([0], near, [], False)
    mine, later = lax.optimization_barrier((mine, messages[1][0]))
    far1 = send(later, flip_perm(count, 8))
    chunks[1], mine = lax.optimization_barrier((chunks[1], mine))
    left = call([1], near, [], False)
    chunks[2], chunks[3], left = lax.optimization_barrier((*chunks[2:], left))
    right = call([2, 3], near, [], False)
    far0, right = lax.optimization_barrier((far0, right))
    far0_sibling = send(far0, flip_perm(count, 1))
    first = [source(far0, 8, 0), source(far0_sibling, 9, 0)]
    rest = call(others, first, [left, right], False)
    far1, rest = lax.optimization_barrier((far1, rest))
    far1_sibling = send(far1, flip_perm(count, 1))
    second = [source(far1, 8, 1), source(far1_sibling, 9, 1)]
    parts = call(others, second, [rest], True)
    back = [send(parts[i], step_perm(count, -steps[i + 1])) for i in range(3)]
    mine = call([0], first + second, [mine], True)[0]
    return combine([mine] + back, tokens, width)


def solution(mesh):
    placed = (
        P("ctx", "head"),
        P("ctx", "head"),
        P("ctx", "head"),
        P("ctx", "head"),
        P("ctx", "head"),
        P(),
        P(),
        P(),
    )
    return jax.shard_map(
        local, mesh=mesh, in_specs=placed, out_specs=P("ctx", "head"), check_vma=False
    )
```

```python
import functools
import math

import jax
import jax.numpy as jnp
from jax import lax
from jax.experimental import pallas as pl
from jax.experimental.pallas import tpu as pltpu
from jax.sharding import PartitionSpec as P

D = 128
BLOCK = 128
SCALE = math.log2(math.e) / math.sqrt(D)
NEG = -1e30
HEADROOM = 40.0
SAFE = 2.0**100
SAMPLE = 256
CUT = 1536
SEGMENT = 512
UNROLL = True
VMEM_LIMIT = 32 * 2**20
NT = (((1,), (1,)), ((), ()))
F32 = jnp.float32
BF16 = jnp.bfloat16


def scores_of(query, keys):
    return lax.dot_general(query, keys, NT, preferred_element_type=F32)


def row_max(x):
    peak = functools.reduce(
        jnp.maximum, [x[:, i : i + D] for i in range(0, x.shape[1], D)]
    )
    return jnp.broadcast_to(jnp.max(peak, axis=1, keepdims=True), (x.shape[0], D))


def attend_kernel(geom, *refs):
    steps, sources, shard, ctx_count, state_in, emit = geom
    n, n_src = len(steps), len(sources)
    kinds, sinks, windows = refs[:3]
    q_in = refs[3 : 3 + n]
    kv = refs[3 + n : 3 + n + n_src]
    rest = refs[3 + n + n_src :]
    old, rest = rest[: len(state_in)], rest[len(state_in) :]
    out, q_buf = rest[0], rest[1]
    state = rest[2] if emit else out
    group = q_in[0].shape[1] // D
    tokens = q_in[0].shape[0]
    q_rows = group * tokens
    ctx = lax.axis_index("ctx")
    head = lax.axis_index("head")
    kind = kinds[head]
    sink = sinks[head]
    window = windows[head]
    total_blocks = ctx_count * shard // BLOCK

    for c in range(n):
        for g in range(group):
            q_buf[c, g * tokens : (g + 1) * tokens, :] = q_in[c][:, g * D : (g + 1) * D]
    with_stretch = [s for s in range(n_src) if sources[s][2]]
    if with_stretch:
        own = sources[with_stretch[0]][2]
        wide = len(with_stretch) * own
        column = lax.broadcasted_iota(jnp.int32, (q_rows, wide), 1)
        token = lax.broadcasted_iota(jnp.int32, (q_rows, wide), 0) % tokens
        key_pos = jnp.zeros_like(column)
        for i, s in enumerate(with_stretch):
            here = (column >= i * own) & (column < (i + 1) * own)
            key_pos = jnp.where(here, (ctx ^ sources[s][0]) * own + column - i * own, key_pos)

    def stretch_parts(c):
        keys, values = [], []
        for s in with_stretch:
            rows = sources[s][1]
            keys.append(kv[s][rows : rows + own, :])
            values.append(kv[s][2 * rows + own : 2 * rows + 2 * own, :])
        owner = jnp.int32(0)
        for i, step in enumerate(steps):
            owner = jnp.where(c == i, source_of(ctx, step), owner)
        x = scores_of(q_buf[c], jnp.concatenate(keys, 0)) * SCALE
        return x, jnp.concatenate(values, 0), key_pos <= token + owner * tokens

    places = [(ref, j) for ref, size in zip(old, state_in) for j in range(size)]

    def restore():
        for c in range(n):
            if state_in:
                ref, j = places[c]
                for i in range(3):
                    state[c, i] = ref[j, i]
            else:
                state[c, 0] = jnp.full((q_rows, D), NEG, F32)
                for i in (1, 2):
                    state[c, i] = jnp.zeros((q_rows, D), F32)

    begin = old[0] if len(state_in) == 1 else state

    def exact(c):
        def update(x, values, mask):
            before = state[c, 0]
            if mask is not None:
                x = jnp.where(mask, x, NEG)
            now = jnp.maximum(before, row_max(x))
            fade = jnp.exp2(before - now)
            total = state[c, 1] * fade
            weights = []
            for j in range(0, x.shape[1], D):
                p = jnp.exp2(x[:, j : j + D] - now)
                if mask is not None:
                    p = jnp.where(mask[:, j : j + D], p, 0.0)
                total = total + p
                weights.append(p.astype(BF16))
            state[c, 0] = now
            state[c, 1] = total
            state[c, 2] = state[c, 2] * fade + jnp.dot(
                jnp.concatenate(weights, 1), values, preferred_element_type=F32
            )

        for s, (flip, rows, extra, first) in enumerate(sources):
            base = (ctx ^ flip) * shard + first
            low = jnp.where(kind == 1, rows, jnp.clip(sink * BLOCK - base, 0, rows))
            high = jnp.clip((total_blocks - window) * BLOCK - base, low, rows)
            span = min(SEGMENT, rows)
            low_end = (low + span - 1) // span
            skip = jnp.maximum(high // span, low_end) - low_end

            def step(j, _, s=s, v_at=rows + extra, low=low, high=high, span=span, low_end=low_end, skip=skip):
                at = pl.multiple_of(jnp.where(j < low_end, j, j + skip) * span, span)
                x = scores_of(q_buf[c], kv[s][pl.ds(at, span), :]) * SCALE
                place = at + lax.broadcasted_iota(jnp.int32, (1, span), 1)
                kept = jnp.broadcast_to((place < low) | (place >= high), x.shape)
                update(x, kv[s][pl.ds(v_at + at, span), :], kept)
                return 0

            lax.fori_loop(0, rows // span - skip, step, 0)
        if with_stretch:
            update(*stretch_parts(c))

    def fixed_stabiliser(chosen):
        segments = []
        for c in range(len(chosen)):
            for s, (_, rows, extra, _) in enumerate(sources):
                for at in range(0, rows, SEGMENT):
                    segments.append((c, s, at, rows + extra + at, min(SEGMENT, rows - at)))
            if with_stretch:
                segments.append((c, None, 0, 0, wide))
        query = [q_buf[c] for c in chosen]
        fixed, total, acc = ([None] * len(chosen) for _ in range(3))
        now = None
        for i in range(len(segments) + 1):
            later = None
            if i < len(segments):
                c, s, at, _, size = segments[i]
                if s is None:
                    later = stretch_parts(chosen[c])
                else:
                    later = (scores_of(query[c], kv[s][at : at + size, :]), None, None)
            if i > 0:
                c, s, _, at, size = segments[i - 1]
                x, values, mask = now
                if s is not None:
                    values = kv[s][at : at + size, :]
                    x = x * SCALE
                if i == 1 or segments[i - 2][0] != c:
                    if state_in:
                        fixed[c], total[c], acc[c] = (begin[chosen[c], k] for k in range(3))
                    else:
                        fixed[c] = row_max(x[:, :SAMPLE]) + HEADROOM
                weights = []
                for j in range(0, size, D):
                    p = jnp.exp2(x[:, j : j + D] - fixed[c])
                    if mask is not None:
                        p = jnp.where(mask[:, j : j + D], p, 0.0)
                    total[c] = p if total[c] is None else total[c] + p
                    weights.append(p.astype(BF16))
                more = jnp.dot(jnp.concatenate(weights, 1), values, preferred_element_type=F32)
                acc[c] = more if acc[c] is None else acc[c] + more
                if i == len(segments) or segments[i][0] != c:
                    state[chosen[c], 0] = fixed[c]
                    state[chosen[c], 1] = total[c]
                    state[chosen[c], 2] = acc[c]
            now = later

    def every_exact():
        if n == 1:
            exact(0)
        else:

            def step(c, _):
                exact(c)
                return 0

            lax.fori_loop(0, n, step, 0)

    def quick():
        if len(state_in) > 1:
            restore()
        if n < 4:
            fixed_stabiliser(list(range(n)))
        else:

            def one(c, _):
                fixed_stabiliser([c])
                return 0

            lax.fori_loop(0, n, one, 0)
        flags = [jnp.where(state[c, 1] < SAFE, 0.0, 1.0) for c in range(n)]
        return jnp.where(jnp.max(functools.reduce(jnp.maximum, flags)) < 0.5, 0, 1)

    left_over = lax.cond(kind == 1, quick, lambda: jnp.int32(1))

    @pl.when(left_over == 1)
    def _():
        restore()
        every_exact()

    if emit:

        def hand_out(c, _):
            total = jnp.sum(state[c, 1], axis=1, keepdims=True)
            some = total > 0.0
            total = jnp.where(some, total, 1.0)
            part = state[c, 2] / total
            out[c, :q_rows, :] = part.astype(BF16)
            log_sum = jnp.where(some, state[c, 0] + jnp.log(total) * math.log2(math.e), NEG)
            eye = lax.broadcasted_iota(jnp.int32, (D, D), 0) == lax.broadcasted_iota(
                jnp.int32, (D, D), 1
            )
            lines = []
            for i in range(0, q_rows, D):
                lines.append(
                    jnp.sum(jnp.where(eye, log_sum[i : i + D, :], 0.0), axis=0, keepdims=True)
                )
            lines = jnp.concatenate(lines, 0)
            pieces = []
            for _ in range(3):
                piece = lines.astype(BF16).astype(F32)
                pieces.append(piece)
                lines = lines - piece
            pad = 16 - 3 * (q_rows // D)
            tail = jnp.concatenate(pieces + [jnp.zeros((pad, D), F32)], 0)
            out[c, q_rows:, :] = tail.astype(BF16)
            return 0

        if n == 1:
            hand_out(0, 0)
        else:
            lax.fori_loop(0, n, hand_out, 0)


def source_of(ctx, step):
    return (ctx // 8) * 8 + (ctx % 8 - 2 * step + 8) % 8


def attend(tables, queries, steps, sources, shard, states, emit):
    n = len(steps)
    tokens, width = queries[0].shape
    q_rows = tokens * (width // D)
    geom = (
        tuple(steps),
        tuple(source[1:] for source in sources),
        shard,
        lax.axis_size("ctx"),
        tuple(array.shape[0] for array in states),
        emit,
    )
    shape_state = (n, 3, q_rows, D)
    if emit:
        out_shape = jax.ShapeDtypeStruct((n, q_rows + 16, D), BF16)
        scratch = [pltpu.VMEM((n, q_rows, D), BF16), pltpu.VMEM(shape_state, F32)]
    else:
        out_shape = jax.ShapeDtypeStruct(shape_state, F32)
        scratch = [pltpu.VMEM((n, q_rows, D), BF16)]
    smem = pl.BlockSpec(memory_space=pltpu.SMEM)
    vmem = pl.BlockSpec(memory_space=pltpu.VMEM)
    pairs = n * q_rows * sum(source[2] + source[3] for source in sources)
    return pl.pallas_call(
        functools.partial(attend_kernel, geom),
        out_shape=out_shape,
        in_specs=[smem] * 3 + [vmem] * (n + len(sources) + len(states)),
        out_specs=vmem,
        scratch_shapes=scratch,
        compiler_params=pltpu.CompilerParams(vmem_limit_bytes=VMEM_LIMIT),
        cost_estimate=pl.CostEstimate(
            flops=4 * pairs * D,
            bytes_accessed=sum(4 * D * (source[2] + source[3]) for source in sources),
            transcendentals=pairs,
        ),
    )(*tables, *queries, *[source[0] for source in sources], *states)


def combine_kernel(*refs):
    *parts, out = refs
    tokens, width = out.shape
    group = width // D
    q_rows = tokens * group
    for i in range(q_rows // D):
        logs = []
        for part in parts:
            tail = part[q_rows:, :].astype(F32)
            step = q_rows // D
            logs.append(
                tail[i : i + 1] + tail[step + i : step + i + 1] + tail[2 * step + i : 2 * step + i + 1]
            )
        peak = functools.reduce(jnp.maximum, logs)
        weights = [jnp.exp2(x - peak) for x in logs]
        total = functools.reduce(jnp.add, weights)
        acc = jnp.zeros((D, D), F32)
        for part, weight in zip(parts, weights):
            spread = jnp.broadcast_to(weight / total, (D, D)).T
            acc = acc + spread * part[i * D : (i + 1) * D, :].astype(F32)
        for j in range(D // tokens):
            g = i * (D // tokens) + j
            out[:, g * D : (g + 1) * D] = acc[j * tokens : (j + 1) * tokens].astype(BF16)


def combine(parts, tokens, width):
    return pl.pallas_call(
        combine_kernel,
        out_shape=jax.ShapeDtypeStruct((tokens, width), BF16),
        compiler_params=pltpu.CompilerParams(vmem_limit_bytes=16 * 2**20),
    )(*parts)


def flip_perm(count, bits):
    return [(i, i ^ bits) for i in range(count)]


def step_perm(count, step):
    return [(i, (i // 8) * 8 + (i % 8 + 2 * step) % 8) for i in range(count)]


def local(
    queries, stretch_keys, stretch_values, cache_keys, cache_values, head_types, sink_blocks, window_blocks
):
    count = lax.axis_size("ctx")
    tables = (head_types, sink_blocks, window_blocks)
    tokens, width = queries.shape
    shard = cache_keys.shape[0]
    own = stretch_keys.shape[0]

    def send(x, perm):
        return lax.ppermute(x, "ctx", perm)

    cut = CUT
    head_part = jnp.concatenate([cache_keys[:cut], cache_values[:cut]], 0)
    tail_part = jnp.concatenate(
        [cache_keys[cut:], stretch_keys, cache_values[cut:], stretch_values], 0
    )
    messages = [(head_part, cut, 0, 0), (tail_part, shard - cut, own, cut)]
    far0 = send(messages[0][0], flip_perm(count, 8))
    steps = [0, 3, 1, 2]
    chunks = [queries] + [send(queries, step_perm(count, s)) for s in steps[1:]]
    sibling = [send(message[0], flip_perm(count, 1)) for message in messages]

    def call(which, sources, states, emit):
        return attend(
            tables, [chunks[i] for i in which], [steps[i] for i in which], sources, shard, states, emit
        )

    def source(array, flip, i):
        return (array, flip) + messages[i][1:]

    near = [source(messages[i][0], 0, i) for i in (0, 1)]
    near += [source(sibling[i], 1, i) for i in (0, 1)]
    others = [1, 2, 3]
    mine = call([0], near, [], False)
    mine, later = lax.optimization_barrier((mine, messages[1][0]))
    far1 = send(later, flip_perm(count, 8))
    chunks[1], mine = lax.optimization_barrier((chunks[1], mine))
    left = call([1], near, [], False)
    chunks[2], chunks[3], left = lax.optimization_barrier((*chunks[2:], left))
    right = call([2, 3], near, [], False)
    far0, right = lax.optimization_barrier((far0, right))
    far0_sibling = send(far0, flip_perm(count, 1))
    first = [source(far0, 8, 0), source(far0_sibling, 9, 0)]
    rest = call(others, first, [left, right], False)
    far1, rest = lax.optimization_barrier((far1, rest))
    far1_sibling = send(far1, flip_perm(count, 1))
    second = [source(far1, 8, 1), source(far1_sibling, 9, 1)]
    parts = call(others, second, [rest], True)
    back = [send(parts[i], step_perm(count, -steps[i + 1])) for i in range(3)]
    mine = call([0], first + second, [mine], True)[0]
    return combine([mine] + back, tokens, width)


def solution(mesh):
    placed = (
        P("ctx", "head"),
        P("ctx", "head"),
        P("ctx", "head"),
        P("ctx", "head"),
        P("ctx", "head"),
        P(),
        P(),
        P(),
    )
    return jax.shard_map(
        local, mesh=mesh, in_specs=placed, out_specs=P("ctx", "head"), check_vma=False
    )
```
